32 devices in a mesh: tm: 4 (over y, x), lon: 8 (over z, core).
Axes of the slice: x: 2, y: 2, z: 4, core: 2. Of those that a mesh axis runs over, the one named last changes fastest.
Arguments:
- first_guess: float32 [8, 64, 80, 64], P('tm', 'lon'), may hold values from -6 to 6
- background: float32 [64, 80, 64], P('lon'), may hold values from -6 to 6
- opening_kernel_matrix: bfloat16 [256, 720], replicated, may hold values from -0.21875 to 0.21875
- hidden_layer_shift: float32 [256], replicated, may hold values from -3 to 3
- closing_kernel_matrix: bfloat16 [80, 2304], replicated, may hold values from -0.125 to 0.125
- output_layer_shift: float32 [80], replicated, may hold values from -2 to 2
- model_weight: float32 [80], replicated, may hold values from 0.5 to 2
- background_weight: float32 [80], replicated, may hold values from 0.5 to 2
- obs_cell: int32 [8, 2048], P('tm', 'lon'), may hold values from 0 to 511
- obs_chan: int32 [8, 2048], P('tm', 'lon'), may hold values from 0 to 79
- obs_value: float32 [8, 2048], P('tm', 'lon'), may hold values from -6 to 6
- obs_weight: float32 [8, 2048], P('tm', 'lon'), may hold values from 0.5 to 4
- step_size: float32 [], replicated, may hold values from 0.3 to 0.6
Outputs:
- analysis: float32 [8, 64, 80, 64], P('tm', 'lon')
- costs: float32 [2], replicated
The draws below stay inside these ranges and needn't reach their ends.
Inputs may be any that keep to these rules, and one draw needn't show every extreme that they name: `obs_cell`: the band of an observation is its column block of 256; the value counts cells of that band, longitude-major.
All inputs are finite; a program needn't handle non-finite values.
Results may differ from the reference program's by a relative error of at most 0.0085.
Values may be sent and summed in bfloat16 or wider, within the bound.
A program may use at most 64 MiB of HBM per device.

```python
import math
import jax
import jax.numpy as jnp
from jax import lax

C = 80
FEAT = 256
LAT = 64
LON_DEV = 8
OBS_DEV = 256
ITERS = 2
NSUB = 8
NLON = 64
OBS = 2048


def set_ends(result, rng, smallest, largest):
    longest = result.shape.index(max(result.shape))
    spots = []
    for shift in (0, 1):
        where = [jax.random.randint(jax.random.fold_in(rng, axis), (), 0, length) for axis, length in enumerate(result.shape)]
        where[longest] = (where[longest] + shift) % result.shape[longest]
        spots.append(tuple(where))
    return result.at[spots[0]].set(smallest).at[spots[1]].set(largest)


def block_scale(key, extent, split, low, high):
    loudness, own = 1.0, jax.random.fold_in(key, 6)
    for position, parts in split:
        heights = jnp.exp(jax.random.uniform(jax.random.fold_in(own, position), (parts,), jnp.float32, low / len(split), high / len(split)))
        loudness = loudness * jnp.repeat(heights, extent[position] // parts).reshape([-1 if axis == position else 1 for axis in range(len(extent))])
    return loudness


def gaussian(own_key, dims, scale, limit, pieces=(), held_as=jnp.bfloat16):
    factor_of = block_scale(own_key, dims, pieces, -0.22, 0.18) if pieces else 1.0
    drawn = jax.random.normal(own_key, dims, jnp.float32) * scale * factor_of
    return jnp.minimum(jnp.maximum(drawn, -limit), limit).astype(held_as)


def setup_inputs(seed: int = 0) -> dict:
    keys = jax.random.split(jax.random.key(seed), 14)
    first_guess = gaussian(keys[0], (NSUB, NLON, C, LAT), 1.0, 6.0, ((0, 4), (1, 8)), jnp.float32)
    background = gaussian(keys[1], (NLON, C, LAT), 1.0, 6.0, ((0, 8),), jnp.float32)
    opening_kernel_matrix = gaussian(keys[2], (FEAT, 9 * C), (9 * C) ** -0.5, 0.21875)
    hidden_layer_shift = gaussian(keys[3], (FEAT,), 0.5, 3.0, (), jnp.float32)
    closing_kernel_matrix = gaussian(keys[4], (C, 9 * FEAT), (9 * FEAT) ** -0.5, 0.125)
    output_layer_shift = gaussian(keys[5], (C,), 0.3, 2.0, (), jnp.float32)
    model_weight = jnp.clip(jnp.exp(jax.random.uniform(keys[6], (C,), jnp.float32, math.log(0.5), math.log(2.0))), 0.5, 2.0)
    background_weight = jnp.clip(jnp.exp(jax.random.uniform(keys[7], (C,), jnp.float32, math.log(0.5), math.log(2.0))), 0.5, 2.0)
    obs_cell = set_ends(jax.random.randint(keys[8], (NSUB, OBS), 0, LON_DEV * LAT), jax.random.fold_in(keys[8], 1), 0, (LON_DEV * LAT) - 1).astype(jnp.int32)
    obs_chan = set_ends(jax.random.randint(keys[9], (NSUB, OBS), 0, C), jax.random.fold_in(keys[9], 1), 0, C - 1).astype(jnp.int32)
    obs_value = gaussian(keys[10], (NSUB, OBS), 1.0, 6.0, ((0, 4), (1, 8)), jnp.float32)
    obs_weight = jnp.clip(jnp.exp(math.log(4.0) - 2.0794415 * jax.random.uniform(keys[11], (NSUB, OBS), jnp.float32) ** block_scale(keys[11], (NSUB, OBS), ((0, 4), (1, 8)), -0.2, 0.2)), 0.5, 4.0)
    step_size = jnp.clip(jax.random.uniform(keys[12], (), jnp.float32, 0.3, 0.6), 0.3, 0.6)
    return dict(first_guess=first_guess, background=background, opening_kernel_matrix=opening_kernel_matrix, hidden_layer_shift=hidden_layer_shift, closing_kernel_matrix=closing_kernel_matrix, output_layer_shift=output_layer_shift, model_weight=model_weight, background_weight=background_weight, obs_cell=obs_cell, obs_chan=obs_chan, obs_value=obs_value, obs_weight=obs_weight, step_size=step_size)


def adjoint_weight(weight):
    rows_out = weight.shape[0]
    rows_in = weight.shape[1] // 9
    flipped = weight.reshape(rows_out, 3, 3, rows_in)[:, ::-1, ::-1, :]
    return flipped.transpose(3, 1, 2, 0).reshape(rows_in, 9 * rows_out)

def wrapped(field):
    return jnp.concatenate([field[-1:], field, field[:1]], axis=0)

def convolve(padded, weight):
    count = padded.shape[0] - 2
    lats = padded.shape[2]
    spread = jnp.pad(padded, ((0, 0), (0, 0), (1, 1)))
    stacked = jnp.concatenate([spread[a:a + count, :, b:b + lats] for a in range(3) for b in range(3)], axis=1)
    return jnp.einsum('fk,nkl->nfl', weight.astype(jnp.float32), stacked.astype(jnp.float32))

def propagate_onestep(system_vector, opening_kernel_matrix, hidden_layer_shift, closing_kernel_matrix, output_layer_shift):
    nonlinear_argument = convolve(wrapped(system_vector.astype(jnp.bfloat16)), opening_kernel_matrix) + hidden_layer_shift[None, :, None]
    hidden = jax.nn.gelu(nonlinear_argument).astype(jnp.bfloat16)
    return (system_vector + convolve(wrapped(hidden), closing_kernel_matrix) + output_layer_shift[None, :, None], nonlinear_argument)

def pullback(cotangent, nonlinear_argument, w_in_adj, w_out_adj):
    inner = convolve(wrapped(cotangent.astype(jnp.bfloat16)), w_out_adj)
    scaled = jax.vjp(jax.nn.gelu, nonlinear_argument)[1](inner)[0].astype(jnp.bfloat16)
    return cotangent + convolve(wrapped(scaled), w_in_adj)

def reference(first_guess, background, opening_kernel_matrix, hidden_layer_shift, closing_kernel_matrix, output_layer_shift, model_weight, background_weight, obs_cell, obs_chan, obs_value, obs_weight, step_size):
    subs, lons, chans, lats = first_guess.shape
    w_in_adj = adjoint_weight(opening_kernel_matrix)
    w_out_adj = adjoint_weight(closing_kernel_matrix)
    model_scale = model_weight[None, None, :, None]
    back_scale = background_weight[:, None]
    column = jnp.arange(obs_cell.shape[1], dtype=jnp.int32)[None, :]
    longitude = column // OBS_DEV * LON_DEV + obs_cell // lats
    flat = (longitude * (chans * lats) + obs_chan * lats + obs_cell % lats).astype(jnp.int32)
    rows = jnp.broadcast_to(jnp.arange(subs, dtype=jnp.int32)[:, None], flat.shape)
    valid = (jnp.arange(subs) > 0).astype(jnp.float32)[:, None, None, None]
    total = float(subs * lons * chans * lats)
    system_vector = first_guess
    costs = []
    for step in range(ITERS):
        propagate_trajectory, nonlinear_argument = lax.map(lambda present_iterate: propagate_onestep(present_iterate, opening_kernel_matrix, hidden_layer_shift, closing_kernel_matrix, output_layer_shift), system_vector)
        earlier_iterate = jnp.concatenate([jnp.zeros_like(propagate_trajectory[:1]), propagate_trajectory[:-1]], axis=0)
        defect = system_vector - earlier_iterate
        forcing = model_scale * defect * valid
        later = jnp.concatenate([forcing[1:], jnp.zeros_like(forcing[:1])], axis=0)
        pulled = lax.map(lambda t: pullback(t[0], t[1], w_in_adj, w_out_adj), (later, nonlinear_argument))
        estimate = jnp.take_along_axis(system_vector.reshape(subs, -1), flat, axis=1)
        misfit = estimate - obs_value
        weighted = obs_weight * misfit
        observed = jnp.zeros((subs, lons * chans * lats), jnp.float32).at[rows, flat].add(weighted).reshape(system_vector.shape)
        departure = system_vector[0] - background
        back_term = jnp.zeros_like(system_vector).at[0].set(back_scale * departure)
        gradient = forcing - pulled + observed + back_term
        cost = 0.5 * (jnp.sum(forcing * defect) + jnp.sum(weighted * misfit) + jnp.sum(back_scale * departure * departure))
        costs.append(cost)
        norm = jnp.sum(gradient * gradient)
        system_vector = system_vector - step_size / jnp.sqrt(norm / total + 1e-06) * gradient
    return (system_vector, jnp.stack(costs))
```

```python
import functools

import jax
import jax.numpy as jnp
from jax import lax
from jax.experimental import pallas as pl
from jax.experimental.pallas import tpu as pltpu
from jax.sharding import PartitionSpec as P

ITERS = 2
F32 = jnp.float32
BF16 = jnp.bfloat16
MESH = pl.DeviceIdType.MESH
ROOT = 0.7978845608028654
CUBE = 0.044715


def column(row):
    n = row.shape[1]
    eye = lax.broadcasted_iota(jnp.int32, (n, n), 0) == lax.broadcasted_iota(jnp.int32, (n, n), 1)
    return jnp.sum(jnp.where(eye, row, 0.0), axis=1, keepdims=True)


def lat_of(n, lats):
    return lax.broadcasted_iota(jnp.int32, (1, n), 1) % lats


def im2col(x, dst, lats):
    chans, n = x.shape
    lat = lat_of(n, lats)
    below = jnp.where(lat == 0, 0.0, pltpu.roll(x, 1, 1))
    above = jnp.where(lat == lats - 1, 0.0, pltpu.roll(x, n - 1, 1))
    for b, v in enumerate((below, x, above)):
        for a, w in enumerate((pltpu.roll(v, lats, 1), v, pltpu.roll(v, n - lats, 1))):
            at = (3 * a + b) * chans
            dst[at : at + chans, :n] = w.astype(BF16)


def stack_lons(src, lo, hi, at, dst, lats):
    feat = src.shape[0]
    n = hi - lo
    two = 2 * lats
    dst[:feat, at : at + n] = pltpu.roll(src[:, lo - two : hi], lats, 1)[:, two:].astype(BF16)
    dst[feat : 2 * feat, at : at + n] = src[:, lo:hi].astype(BF16)
    dst[2 * feat :, at : at + n] = pltpu.roll(src[:, lo : hi + two], n + two - lats, 1)[:, :n].astype(BF16)


def sum_lats(p, lats):
    chans = p.shape[0] // 3
    n = p.shape[1]
    lat = lat_of(n, lats)
    below = jnp.where(lat == 0, 0.0, pltpu.roll(p[:chans], 1, 1))
    above = jnp.where(lat == lats - 1, 0.0, pltpu.roll(p[2 * chans :], n - 1, 1))
    return p[chans : 2 * chans] + below + above


def folded(v):
    acc = v[:, :128]
    for i in range(1, v.shape[1] // 128):
        acc = acc + v[:, 128 * i : 128 * (i + 1)]
    tile = acc[:8]
    for i in range(1, acc.shape[0] // 8):
        tile = tile + acc[8 * i : 8 * (i + 1)]
    return tile


def chunks(lo, hi, size=256):
    return [(c, min(c + size, hi)) for c in range(lo, hi, size)]


def kernel(
    total, tms, lons,
    fg, bg, w1, b1, w2, b2, mw, bw, cell, chan, val, wt, step,
    out, costs,
    xe, rx, sx, sten, hf, hs, gp, qf, mx, lx, gx, ow, ov, v2, w1p, v1p, tall, wide,
    ms, mr, ar1, ar2,
    halo_send, halo_recv, m_send, m_recv, a1_send, a1_recv, a2_send, a2_recv,
):
    subs, band, chans, lats = fg.shape
    feat = w1.shape[0]
    own = band * lats
    lo, hi = 4 * lats, 4 * lats + own
    wlo, whi = 2 * lats, 6 * lats + own
    ext = hi + 4 * lats
    win = whi - wlo
    t = lax.axis_index("tm")
    l = lax.axis_index("lon")
    tp, tn = lax.rem(t + tms - 1, tms), lax.rem(t + 1, tms)
    ll, lr = lax.rem(l + lons - 1, lons), lax.rem(l + 1, lons)
    lon_peers = [lax.rem(l + d, lons) for d in range(1, lons)]
    tm_peers = [lax.rem(t + d, tms) for d in range(1, tms)]

    barrier = pltpu.get_barrier_semaphore()
    for peer in lon_peers:
        pl.semaphore_signal(barrier, inc=1, device_id=(t, peer), device_id_type=MESH)
    for peer in tm_peers:
        pl.semaphore_signal(barrier, inc=1, device_id=(peer, l), device_id_type=MESH)
    for peer in (ll, lr):
        pl.semaphore_signal(barrier, inc=1, device_id=(tn, peer), device_id_type=MESH)

    def halo_copies(it):
        src, dst = sx.at[it], rx.at[it]
        four, two = 4 * lats, 2 * lats
        first = slice(0, 1)
        parts = (
            (src.at[:, :, own - four :], dst.at[:subs, :, :lo], (t, lr)),
            (src.at[:, :, :four], dst.at[:subs, :, hi:], (t, ll)),
            (src.at[first], dst.at[subs:, :, lo:hi], (tp, l)),
            (src.at[first, :, own - two :], dst.at[subs:, :, wlo:lo], (tp, lr)),
            (src.at[first, :, :two], dst.at[subs:, :, hi:whi], (tp, ll)),
        )
        return [
            pltpu.make_async_remote_copy(
                src_ref=s, dst_ref=d, send_sem=halo_send.at[it, i], recv_sem=halo_recv.at[it, i],
                device_id=dev, device_id_type=MESH,
            )
            for i, (s, d, dev) in enumerate(parts)
        ]

    for s in range(subs):
        for i in range(0, band, 2):
            pair = jnp.concatenate([fg[s, i], fg[s, i + 1]], axis=1)
            xe[s, :, lo + i * lats : lo + (i + 2) * lats] = pair
            sx[0, s, :, i * lats : (i + 2) * lats] = pair.astype(BF16)
    pl.semaphore_wait(barrier, lons - 1 + tms - 1 + 2)
    pending = []
    halos = halo_copies(0)
    for c in halos:
        c.start()

    for a in range(3):
        for b in range(3):
            block = w2[:, (3 * a + b) * feat : (3 * a + b + 1) * feat]
            v2[b * chans : (b + 1) * chans, a * feat : (a + 1) * feat] = block
            at = (3 * (2 - a) + (2 - b)) * chans
            tall[at : at + chans, :] = block.astype(F32)
    tall[9 * chans :, :] = jnp.zeros((tall.shape[0] - 9 * chans, feat), F32)
    w1p[...] = jnp.transpose(tall[...]).astype(BF16)
    wide[:, wide.shape[1] - 128 :] = jnp.zeros((feat, 128), F32)
    wide[:, : 9 * chans] = w1[...].astype(F32)
    tall[...] = jnp.transpose(wide[...])
    for a in range(3):
        for b in range(3):
            at = (3 * (2 - a) + (2 - b)) * chans
            v1p[b * chans : (b + 1) * chans, a * feat : (a + 1) * feat] = tall[at : at + chans, :].astype(BF16)
    b1c, b2c, mwc, bwc = column(b1[...]), column(b2[...]), column(mw[...]), column(bw[...])

    fixed = jnp.zeros((), F32)
    nobs = cell.shape[1]
    for s in range(subs):
        weight, value = wt[s : s + 1, :], val[s : s + 1, :]
        fixed = fixed + jnp.sum(weight * value * value)
        at_chan = lax.broadcasted_iota(jnp.int32, (chans, nobs), 0) == chan[s : s + 1, :]
        at_cell = (lax.broadcasted_iota(jnp.int32, (own, nobs), 0) == cell[s : s + 1, :]).astype(F32).astype(BF16)
        for quantity, dst in ((weight, ow), (weight * value, ov)):
            rest, rows = quantity, []
            for _ in range(3):
                part = rest.astype(BF16).astype(F32)
                rest = rest - part
                rows.append(jnp.where(at_chan, part, 0.0).astype(BF16))
            spread = lax.dot_general(
                jnp.concatenate(rows, axis=0), at_cell, (((1,), (1,)), ((), ())), preferred_element_type=F32
            )
            dst[s] = spread[:chans] + spread[chans : 2 * chans] + spread[2 * chans :]

    starts = (t > 0).astype(F32)
    ends = (t < tms - 1).astype(F32)
    anchor = (t == 0).astype(F32)
    origin = lax.broadcasted_iota(jnp.int32, (8, 128), 0) * 128 + lax.broadcasted_iota(jnp.int32, (8, 128), 1) == 0

    alpha = None
    for it in range(ITERS):
        for c in halos:
            c.wait_recv()
        pending += halos
        for s in range(subs + 1):
            for x0, x1 in ((0, lo), (hi, ext)) if s < subs else ((wlo, whi),):
                got = rx[it, s, :, x0:x1].astype(F32)
                xe[s, :, x0:x1] = got if it == 0 else xe[s, :, x0:x1] - alpha * got

        for s in reversed(range(subs)):
            im2col(xe[s], sten, lats)
            for c0, c1 in chunks(0, ext):
                pre = jnp.dot(w1[...], sten[:, c0:c1], preferred_element_type=F32) + b1c
                sq = pre * pre
                th = jnp.tanh(ROOT * pre * (1.0 + CUBE * sq))
                half = 0.5 * (1.0 + th)
                hf[:, c0:c1] = pre * half
                slope = half + (0.5 * ROOT) * pre * (1.0 - th * th) * (1.0 + 3.0 * CUBE * sq)
                gp[s, :, c0:c1] = slope
            for c0, c1 in chunks(wlo, whi):
                stack_lons(hf, c0, c1, c0 - wlo, hs, lats)
                p = jnp.dot(v2[...], hs[:, c0 - wlo : c1 - wlo], preferred_element_type=F32)
                mx[s, :, c0 - wlo : c1 - wlo] = xe[s, :, c0:c1] + sum_lats(p, lats) + b2c
            if s == subs - 1:
                ms[it] = mx[s, :, lo - wlo : hi - wlo].astype(BF16)
                m_copy = pltpu.make_async_remote_copy(
                    src_ref=ms.at[it], dst_ref=mr.at[it], send_sem=m_send.at[it], recv_sem=m_recv.at[it],
                    device_id=(tn, l), device_id_type=MESH,
                )
                m_copy.start()
                pending.append(m_copy)

        for s in range(subs):
            scale = mwc if s < subs - 1 else mwc * ends
            lx[s + 1] = scale * (xe[s + 1, :, wlo:whi] - mx[s])

        norm = jnp.zeros((8, 128), F32)
        cost = jnp.where(origin, fixed, 0.0)
        for s in reversed(range(subs)):
            im2col(lx[s + 1], sten, lats)
            for c0, c1 in chunks(0, win):
                z = jnp.dot(w1p[:, : 9 * chans], sten[:, c0:c1], preferred_element_type=F32)
                qf[:, c0:c1] = gp[s, :, wlo + c0 : wlo + c1] * z
            pulled = []
            for c0, c1 in chunks(lo - wlo, hi - wlo):
                at = c0 - (lo - wlo)
                stack_lons(qf, c0, c1, at, hs, lats)
                p = jnp.dot(v1p[...], hs[:, at : at + c1 - c0], preferred_element_type=F32)
                pulled.append(lx[s + 1, :, c0:c1] + sum_lats(p, lats))
            pulled = jnp.concatenate(pulled, axis=1)
            x = xe[s, :, lo:hi]
            if s > 0:
                forcing = lx[s, :, lo - wlo : hi - wlo]
                defect = x - mx[s - 1, :, lo - wlo : hi - wlo]
            else:
                m_copy.wait_recv()
                defect = x - mr[it].astype(F32)
                forcing = (mwc * starts) * defect
            weighted = ow[s] * x - ov[s]
            cost = cost + folded(forcing * defect + (weighted - ov[s]) * x)
            g = forcing - pulled + weighted
            if s == 0:
                back = jnp.concatenate([bg[i] for i in range(band)], axis=1)
                departure = x - back
                pull = (bwc * anchor) * departure
                cost = cost + folded(pull * departure)
                g = g + pull
            norm = norm + folded(g * g)
            gx[s] = g
            if it < ITERS - 1:
                sx[it + 1, s] = g.astype(BF16)

        ar1[it, l, :8] = norm
        ar1[it, l, 8:] = cost
        first_phase = [
            pltpu.make_async_remote_copy(
                src_ref=ar1.at[it, l], dst_ref=ar1.at[it, l], send_sem=a1_send.at[it, i], recv_sem=a1_recv.at[it, i],
                device_id=(t, peer), device_id_type=MESH,
            )
            for i, peer in enumerate(lon_peers)
        ]
        for c in first_phase:
            c.start()
        if it < ITERS - 1:
            halos = halo_copies(it + 1)
            for c in halos:
                c.start()
        for c in first_phase:
            c.wait_recv()
        ar2[it, t] = functools.reduce(jnp.add, [ar1[it, i] for i in range(lons)])
        second_phase = [
            pltpu.make_async_remote_copy(
                src_ref=ar2.at[it, t], dst_ref=ar2.at[it, t], send_sem=a2_send.at[it, i], recv_sem=a2_recv.at[it, i],
                device_id=(peer, l), device_id_type=MESH,
            )
            for i, peer in enumerate(tm_peers)
        ]
        for c in second_phase:
            c.start()
        for c in second_phase:
            c.wait_recv()
        pending += first_phase + second_phase
        both = functools.reduce(jnp.add, [ar2[it, i] for i in range(tms)])
        costs[it] = 0.5 * jnp.sum(both[8:])
        sum_sq = jnp.sum(jnp.sum(both[:8], axis=0, keepdims=True), axis=1, keepdims=True)
        alpha = step[...] / jnp.sqrt(sum_sq / total + 1e-06)
        for s in range(subs):
            x = xe[s, :, lo:hi] - alpha * gx[s]
            if it < ITERS - 1:
                xe[s, :, lo:hi] = x
            else:
                for i in range(band):
                    out[s, i] = x[:, i * lats : (i + 1) * lats]
    for c in pending:
        c.wait_send()


def per_device(fg, bg, w1, b1, w2, b2, mw, bw, cell, chan, val, wt, step):
    subs, band, chans, lats = fg.shape
    feat = w1.shape[0]
    tms, lons = lax.axis_size("tm"), lax.axis_size("lon")
    total = float(subs * tms * band * lons * chans * lats)
    own = band * lats
    win = own + 4 * lats
    ext = own + 8 * lats
    rows = -(-9 * chans // 128) * 128
    vmem = pl.BlockSpec(memory_space=pltpu.VMEM)
    dma = pltpu.SemaphoreType.DMA
    return pl.pallas_call(
        functools.partial(kernel, total, tms, lons),
        out_shape=(
            jax.ShapeDtypeStruct(fg.shape, F32),
            jax.ShapeDtypeStruct((ITERS,), F32),
        ),
        in_specs=[vmem] * 13,
        out_specs=(vmem, pl.BlockSpec(memory_space=pltpu.SMEM)),
        scratch_shapes=[
            pltpu.VMEM((subs + 1, chans, ext), F32),
            pltpu.VMEM((ITERS, subs + 1, chans, ext), BF16),
            pltpu.VMEM((ITERS, subs, chans, own), BF16),
            pltpu.VMEM((9 * chans, ext), BF16),
            pltpu.VMEM((feat, ext), F32),
            pltpu.VMEM((3 * feat, win), BF16),
            pltpu.VMEM((subs, feat, ext), F32),
            pltpu.VMEM((feat, win), F32),
            pltpu.VMEM((subs, chans, win), F32),
            pltpu.VMEM((subs + 1, chans, win), F32),
            pltpu.VMEM((subs, chans, own), F32),
            pltpu.VMEM((subs, chans, own), F32),
            pltpu.VMEM((subs, chans, own), F32),
            pltpu.VMEM((3 * chans, 3 * feat), BF16),
            pltpu.VMEM((feat, rows), BF16),
            pltpu.VMEM((3 * chans, 3 * feat), BF16),
            pltpu.VMEM((rows, feat), F32),
            pltpu.VMEM((feat, rows), F32),
            pltpu.VMEM((ITERS, chans, own), BF16),
            pltpu.VMEM((ITERS, chans, own), BF16),
            pltpu.VMEM((ITERS, lons, 16, 128), F32),
            pltpu.VMEM((ITERS, tms, 16, 128), F32),
            dma((ITERS, 5)),
            dma((ITERS, 5)),
            dma((ITERS,)),
            dma((ITERS,)),
            dma((ITERS, lons - 1)),
            dma((ITERS, lons - 1)),
            dma((ITERS, tms - 1)),
            dma((ITERS, tms - 1)),
        ],
        compiler_params=pltpu.CompilerParams(
            collective_id=0, has_side_effects=True, vmem_limit_bytes=48 * 1024 * 1024
        ),
    )(
        fg, bg, w1, b1.reshape(1, -1), w2, b2.reshape(1, -1), mw.reshape(1, -1), bw.reshape(1, -1),
        cell, chan, val, wt, step.reshape(1, 1),
    )


def solution(mesh):
    in_specs = (
        P("tm", "lon", None, None),
        P("lon", None, None),
        P(),
        P(),
        P(),
        P(),
        P(),
        P(),
        P("tm", "lon"),
        P("tm", "lon"),
        P("tm", "lon"),
        P("tm", "lon"),
        P(),
    )
    out_specs = (P("tm", "lon", None, None), P())
    return jax.shard_map(
        per_device, mesh=mesh, in_specs=in_specs, out_specs=out_specs, check_vma=False
    )
```

```python
import functools

import jax
import jax.numpy as jnp
from jax import lax
from jax.experimental import pallas as pl
from jax.experimental.pallas import tpu as pltpu
from jax.sharding import PartitionSpec as P

ITERS = 2
F32 = jnp.float32
BF16 = jnp.bfloat16
MESH = pl.DeviceIdType.MESH
ROOT = 0.7978845608028654
CUBE = 0.044715


def column(row):
    n = row.shape[1]
    eye = lax.broadcasted_iota(jnp.int32, (n, n), 0) == lax.broadcasted_iota(jnp.int32, (n, n), 1)
    return jnp.sum(jnp.where(eye, row, 0.0), axis=1, keepdims=True)


def lat_of(n, lats):
    return lax.broadcasted_iota(jnp.int32, (1, n), 1) % lats


def im2col(x, dst, lats):
    chans, n = x.shape
    lat = lat_of(n, lats)
    below = jnp.where(lat == 0, 0.0, pltpu.roll(x, 1, 1))
    above = jnp.where(lat == lats - 1, 0.0, pltpu.roll(x, n - 1, 1))
    for b, wide in enumerate((below, x, above)):
        v = wide.astype(BF16)
        for a, w in enumerate((pltpu.roll(v, lats, 1), v, pltpu.roll(v, n - lats, 1))):
            at = (3 * a + b) * chans
            dst[at : at + chans, :n] = w


def stack_lons(src, lo, hi, at, dst, lats):
    feat = src.shape[0]
    n = hi - lo
    two = 2 * lats
    dst[:feat, at : at + n] = pltpu.roll(src[:, lo - two : hi], lats, 1)[:, two:]
    dst[feat : 2 * feat, at : at + n] = src[:, lo:hi]
    dst[2 * feat :, at : at + n] = pltpu.roll(src[:, lo : hi + two], n + two - lats, 1)[:, :n]


def sum_lats(p, lats):
    chans = p.shape[0] // 3
    n = p.shape[1]
    lat = lat_of(n, lats)
    below = jnp.where(lat == 0, 0.0, pltpu.roll(p[:chans], 1, 1))
    above = jnp.where(lat == lats - 1, 0.0, pltpu.roll(p[2 * chans :], n - 1, 1))
    return p[chans : 2 * chans] + below + above


def folded(v):
    acc = v[:, :128]
    for i in range(1, v.shape[1] // 128):
        acc = acc + v[:, 128 * i : 128 * (i + 1)]
    tile = acc[:8]
    for i in range(1, acc.shape[0] // 8):
        tile = tile + acc[8 * i : 8 * (i + 1)]
    return tile


def chunks(lo, hi, size=256):
    return [(c, min(c + size, hi)) for c in range(lo, hi, size)]


def kernel(
    total, tms, lons, lats,
    fg, bg, w1t, b1, w2, b2, mw, bw, cell, chan, val, wt, step,
    out, costs,
    xe, rx, sx, sten, hf, hs, gp, qf, mx, lx, gx, ow, ov, v2, w1s, w1p, v1p, tall, tall1, pp, cg,
    ms, mr, ar1, ar2,
    halo_send, halo_recv, m_send, m_recv, a1_send, a1_recv, a2_send, a2_recv,
):
    subs, own, chans = fg.shape
    feat = w1t.shape[1]
    lo, hi = 4 * lats, 4 * lats + own
    wlo, whi = 2 * lats, 6 * lats + own
    ext = hi + 4 * lats
    win = whi - wlo
    t = lax.axis_index("tm")
    l = lax.axis_index("lon")
    tp, tn = lax.rem(t + tms - 1, tms), lax.rem(t + 1, tms)
    ll, lr = lax.rem(l + lons - 1, lons), lax.rem(l + 1, lons)
    lon_peers = [lax.rem(l + d, lons) for d in range(1, lons)]
    tm_peers = [lax.rem(t + d, tms) for d in range(1, tms)]

    barrier = pltpu.get_barrier_semaphore()
    for peer in lon_peers:
        pl.semaphore_signal(barrier, inc=1, device_id=(t, peer), device_id_type=MESH)
    for peer in tm_peers:
        pl.semaphore_signal(barrier, inc=1, device_id=(peer, l), device_id_type=MESH)
    for peer in (ll, lr):
        pl.semaphore_signal(barrier, inc=1, device_id=(tn, peer), device_id_type=MESH)

    def halo_copies(it):
        src, dst = sx.at[it], rx.at[it]
        four, two = 4 * lats, 2 * lats
        first = slice(0, 1)
        parts = (
            (src.at[:, :, own - four :], dst.at[:subs, :, :lo], (t, lr)),
            (src.at[:, :, :four], dst.at[:subs, :, hi:], (t, ll)),
            (src.at[first], dst.at[subs:, :, lo:hi], (tp, l)),
            (src.at[first, :, own - two :], dst.at[subs:, :, wlo:lo], (tp, lr)),
            (src.at[first, :, :two], dst.at[subs:, :, hi:whi], (tp, ll)),
        )
        return [
            pltpu.make_async_remote_copy(
                src_ref=s, dst_ref=d, send_sem=halo_send.at[it, i], recv_sem=halo_recv.at[it, i],
                device_id=dev, device_id_type=MESH,
            )
            for i, (s, d, dev) in enumerate(parts)
        ]

    for s in range(subs):
        x = jnp.transpose(fg[s])
        xe[s, :, lo:hi] = x
        sx[0, s] = x.astype(BF16)
    pl.semaphore_wait(barrier, lons - 1 + tms - 1 + 2)
    pending = []
    halos = halo_copies(0)
    for c in halos:
        c.start()

    for a in range(3):
        for b in range(3):
            block = w2[:, (3 * a + b) * feat : (3 * a + b + 1) * feat]
            v2[b * chans : (b + 1) * chans, a * feat : (a + 1) * feat] = block
            at = (3 * (2 - a) + (2 - b)) * chans
            tall[at : at + chans, :] = block.astype(F32)
    tall[9 * chans :, :] = jnp.zeros((tall.shape[0] - 9 * chans, feat), F32)
    w1p[...] = jnp.transpose(tall[...]).astype(BF16)
    tall1[: 9 * chans, :] = w1t[...].astype(F32)
    tall1[9 * chans :, :] = jnp.zeros((tall1.shape[0] - 9 * chans, feat), F32)
    w1s[...] = jnp.transpose(tall1[...]).astype(BF16)
    for a in range(3):
        for b in range(3):
            at = (3 * (2 - a) + (2 - b)) * chans
            v1p[b * chans : (b + 1) * chans, a * feat : (a + 1) * feat] = w1t[at : at + chans, :]
    b1c, b2c, mwc, bwc = column(b1[...]), column(b2[...]), column(mw[...]), column(bw[...])

    fixed = jnp.zeros((), F32)
    nobs = cell.shape[1]
    for s in range(subs):
        weight, value = wt[s : s + 1, :], val[s : s + 1, :]
        fixed = fixed + jnp.sum(weight * value * value)
        at_chan = lax.broadcasted_iota(jnp.int32, (chans, nobs), 0) == chan[s : s + 1, :]
        at_cell = (lax.broadcasted_iota(jnp.int32, (own, nobs), 0) == cell[s : s + 1, :]).astype(F32).astype(BF16)
        for quantity, dst in ((weight, ow), (weight * value, ov)):
            rest, rows = quantity, []
            for _ in range(3):
                part = rest.astype(BF16).astype(F32)
                rest = rest - part
                rows.append(jnp.where(at_chan, part, 0.0).astype(BF16))
            spread = lax.dot_general(
                jnp.concatenate(rows, axis=0), at_cell, (((1,), (1,)), ((), ())), preferred_element_type=F32
            )
            dst[s] = spread[:chans] + spread[chans : 2 * chans] + spread[2 * chans :]

    starts = (t > 0).astype(F32)
    ends = (t < tms - 1).astype(F32)
    anchor = (t == 0).astype(F32)
    origin = lax.broadcasted_iota(jnp.int32, (8, 128), 0) * 128 + lax.broadcasted_iota(jnp.int32, (8, 128), 1) == 0

    alpha = None
    for it in range(ITERS):
        if it == 0:
            for c in halos:
                c.wait_recv()
        pending += halos
        for s in range(subs + 1):
            for x0, x1 in ((0, lo), (hi, ext)) if s < subs else ((wlo, whi),):
                got = rx[it, s, :, x0:x1].astype(F32)
                xe[s, :, x0:x1] = got if it == 0 else xe[s, :, x0:x1] - alpha * got

        for s in reversed(range(subs)):
            if it == 0:
                im2col(xe[s], sten, lats)
            for c0, c1 in chunks(0, ext):
                if it == 0:
                    pre = jnp.dot(w1s[:, : 9 * chans], sten[:, c0:c1], preferred_element_type=F32) + b1c
                else:
                    pre = pp[s, :, c0:c1] - alpha * cg[s, :, c0:c1]
                if it < ITERS - 1:
                    pp[s, :, c0:c1] = pre
                sq = pre * pre
                half = 0.5 + 0.5 * jnp.tanh(pre * (ROOT + (ROOT * CUBE) * sq))
                hid = pre * half
                hf[:, c0:c1] = hid.astype(BF16)
                gp[s, :, c0:c1] = half + hid * (1.0 - half) * (2.0 * ROOT + (6.0 * ROOT * CUBE) * sq)
            for c0, c1 in chunks(wlo, whi):
                stack_lons(hf, c0, c1, c0 - wlo, hs, lats)
                p = jnp.dot(v2[...], hs[:, c0 - wlo : c1 - wlo], preferred_element_type=F32)
                mx[s, :, c0 - wlo : c1 - wlo] = xe[s, :, c0:c1] + sum_lats(p, lats) + b2c
            if s == subs - 1:
                ms[it] = mx[s, :, lo - wlo : hi - wlo].astype(BF16)
                m_copy = pltpu.make_async_remote_copy(
                    src_ref=ms.at[it], dst_ref=mr.at[it], send_sem=m_send.at[it], recv_sem=m_recv.at[it],
                    device_id=(tn, l), device_id_type=MESH,
                )
                m_copy.start()
                pending.append(m_copy)

        for s in range(subs):
            scale = mwc if s < subs - 1 else mwc * ends
            lx[s + 1] = scale * (xe[s + 1, :, wlo:whi] - mx[s])

        norm = jnp.zeros((8, 128), F32)
        cost = jnp.where(origin, fixed, 0.0)
        for s in reversed(range(subs)):
            im2col(lx[s + 1], sten, lats)
            for c0, c1 in chunks(0, win):
                z = jnp.dot(w1p[:, : 9 * chans], sten[:, c0:c1], preferred_element_type=F32)
                qf[:, c0:c1] = (gp[s, :, wlo + c0 : wlo + c1] * z).astype(BF16)
            pulled = []
            for c0, c1 in chunks(lo - wlo, hi - wlo):
                at = c0 - (lo - wlo)
                stack_lons(qf, c0, c1, at, hs, lats)
                p = jnp.dot(v1p[...], hs[:, at : at + c1 - c0], preferred_element_type=F32)
                pulled.append(lx[s + 1, :, c0:c1] + sum_lats(p, lats))
            pulled = jnp.concatenate(pulled, axis=1)
            x = xe[s, :, lo:hi]
            if s > 0:
                forcing = lx[s, :, lo - wlo : hi - wlo]
                defect = x - mx[s - 1, :, lo - wlo : hi - wlo]
            else:
                m_copy.wait_recv()
                defect = x - mr[it].astype(F32)
                forcing = (mwc * starts) * defect
            weighted = ow[s] * x - ov[s]
            cost = cost + folded(forcing * defect + (weighted - ov[s]) * x)
            g = forcing - pulled + weighted
            if s == 0:
                back = jnp.transpose(bg[...])
                departure = x - back
                pull = (bwc * anchor) * departure
                cost = cost + folded(pull * departure)
                g = g + pull
            norm = norm + folded(g * g)
            gx[s] = g
            if it < ITERS - 1:
                sx[it + 1, s] = g.astype(BF16)

        ar1[it, l, :8] = norm
        ar1[it, l, 8:] = cost
        first_phase = [
            pltpu.make_async_remote_copy(
                src_ref=ar1.at[it, l], dst_ref=ar1.at[it, l], send_sem=a1_send.at[it, i], recv_sem=a1_recv.at[it, i],
                device_id=(t, peer), device_id_type=MESH,
            )
            for i, peer in enumerate(lon_peers)
        ]
        for c in first_phase:
            c.start()
        if it < ITERS - 1:
            halos = halo_copies(it + 1)
            for c in halos:
                c.start()
        for c in first_phase:
            c.wait_recv()
        ar2[it, t] = functools.reduce(jnp.add, [ar1[it, i] for i in range(lons)])
        second_phase = [
            pltpu.make_async_remote_copy(
                src_ref=ar2.at[it, t], dst_ref=ar2.at[it, t], send_sem=a2_send.at[it, i], recv_sem=a2_recv.at[it, i],
                device_id=(peer, l), device_id_type=MESH,
            )
            for i, peer in enumerate(tm_peers)
        ]
        for c in second_phase:
            c.start()
        if it < ITERS - 1:
            for c in halos:
                c.wait_recv()
            for s in range(subs):
                left, right = rx[it + 1, s, :, :lo].astype(F32), rx[it + 1, s, :, hi:].astype(F32)
                im2col(jnp.concatenate([left, gx[s], right], axis=1), sten, lats)
                for c0, c1 in chunks(0, ext):
                    cg[s, :, c0:c1] = jnp.dot(
                        w1s[:, : 9 * chans], sten[:, c0:c1], preferred_element_type=F32
                    )
        for c in second_phase:
            c.wait_recv()
        pending += first_phase + second_phase
        both = functools.reduce(jnp.add, [ar2[it, i] for i in range(tms)])
        costs[it] = 0.5 * jnp.sum(both[8:])
        sum_sq = jnp.sum(jnp.sum(both[:8], axis=0, keepdims=True), axis=1, keepdims=True)
        alpha = step[...] / jnp.sqrt(sum_sq / total + 1e-06)
        for s in range(subs):
            x = xe[s, :, lo:hi] - alpha * gx[s]
            if it < ITERS - 1:
                xe[s, :, lo:hi] = x
            else:
                out[s] = jnp.transpose(x)
    for c in pending:
        c.wait_send()


def per_device(fg, bg, w1, b1, w2, b2, mw, bw, cell, chan, val, wt, step):
    subs, band, chans, lats = fg.shape
    feat = w1.shape[0]
    tms, lons = lax.axis_size("tm"), lax.axis_size("lon")
    total = float(subs * tms * band * lons * chans * lats)
    own = band * lats
    win = own + 4 * lats
    ext = own + 8 * lats
    rows = -(-9 * chans // 128) * 128
    vmem = pl.BlockSpec(memory_space=pltpu.VMEM)
    dma = pltpu.SemaphoreType.DMA
    analysis, costs = pl.pallas_call(
        functools.partial(kernel, total, tms, lons, lats),
        out_shape=(
            jax.ShapeDtypeStruct((subs, own, chans), F32),
            jax.ShapeDtypeStruct((ITERS,), F32),
        ),
        in_specs=[vmem] * 13,
        out_specs=(vmem, pl.BlockSpec(memory_space=pltpu.SMEM)),
        scratch_shapes=[
            pltpu.VMEM((subs + 1, chans, ext), F32),
            pltpu.VMEM((ITERS, subs + 1, chans, ext), BF16),
            pltpu.VMEM((ITERS, subs, chans, own), BF16),
            pltpu.VMEM((9 * chans, ext), BF16),
            pltpu.VMEM((feat, ext), BF16),
            pltpu.VMEM((3 * feat, win), BF16),
            pltpu.VMEM((subs, feat, ext), F32),
            pltpu.VMEM((feat, win), BF16),
            pltpu.VMEM((subs, chans, win), F32),
            pltpu.VMEM((subs + 1, chans, win), F32),
            pltpu.VMEM((subs, chans, own), F32),
            pltpu.VMEM((subs, chans, own), F32),
            pltpu.VMEM((subs, chans, own), F32),
            pltpu.VMEM((3 * chans, 3 * feat), BF16),
            pltpu.VMEM((feat, rows), BF16),
            pltpu.VMEM((feat, rows), BF16),
            pltpu.VMEM((3 * chans, 3 * feat), BF16),
            pltpu.VMEM((rows, feat), F32),
            pltpu.VMEM((rows, feat), F32),
            pltpu.VMEM((subs, feat, ext), F32),
            pltpu.VMEM((subs, feat, ext), F32),
            pltpu.VMEM((ITERS, chans, own), BF16),
            pltpu.VMEM((ITERS, chans, own), BF16),
            pltpu.VMEM((ITERS, lons, 16, 128), F32),
            pltpu.VMEM((ITERS, tms, 16, 128), F32),
            dma((ITERS, 5)),
            dma((ITERS, 5)),
            dma((ITERS,)),
            dma((ITERS,)),
            dma((ITERS, lons - 1)),
            dma((ITERS, lons - 1)),
            dma((ITERS, tms - 1)),
            dma((ITERS, tms - 1)),
        ],
        compiler_params=pltpu.CompilerParams(
            collective_id=0, has_side_effects=True, vmem_limit_bytes=48 * 1024 * 1024
        ),
    )(
        jnp.swapaxes(fg, 2, 3).reshape(subs, own, chans), jnp.swapaxes(bg, 1, 2).reshape(own, chans), w1.T, b1.reshape(1, -1), w2, b2.reshape(1, -1), mw.reshape(1, -1), bw.reshape(1, -1),
        cell, chan, val, wt, step.reshape(1, 1),
    )
    return jnp.swapaxes(analysis.reshape(subs, band, lats, chans), 2, 3), costs


def solution(mesh):
    in_specs = (
        P("tm", "lon", None, None),
        P("lon", None, None),
        P(),
        P(),
        P(),
        P(),
        P(),
        P(),
        P("tm", "lon"),
        P("tm", "lon"),
        P("tm", "lon"),
        P("tm", "lon"),
        P(),
    )
    out_specs = (P("tm", "lon", None, None), P())
    return jax.shard_map(
        per_device, mesh=mesh, in_specs=in_specs, out_specs=out_specs, check_vma=False
    )
```

```python
import functools

import jax
import jax.numpy as jnp
from jax import lax
from jax.experimental import pallas as pl
from jax.experimental.pallas import tpu as pltpu
from jax.sharding import PartitionSpec as P

ITERS = 2
F32 = jnp.float32
BF16 = jnp.bfloat16
MESH = pl.DeviceIdType.MESH
ROOT = 0.7978845608028654
CUBE = 0.044715


def column(row):
    n = row.shape[1]
    eye = lax.broadcasted_iota(jnp.int32, (n, n), 0) == lax.broadcasted_iota(jnp.int32, (n, n), 1)
    return jnp.sum(jnp.where(eye, row, 0.0), axis=1, keepdims=True)


def lat_of(n, lats):
    return lax.broadcasted_iota(jnp.int32, (1, n), 1) % lats


def im2col(x, dst, lats):
    chans, n = x.shape
    lat = lat_of(n, lats)
    below = jnp.where(lat == 0, 0.0, pltpu.roll(x, 1, 1))
    above = jnp.where(lat == lats - 1, 0.0, pltpu.roll(x, n - 1, 1))
    for b, wide in enumerate((below, x, above)):
        v = wide.astype(BF16)
        for a, w in enumerate((pltpu.roll(v, lats, 1), v, pltpu.roll(v, n - lats, 1))):
            at = (3 * a + b) * chans
            dst[at : at + chans, :n] = w


def stack_lons(src, lo, hi, at, dst, lats):
    feat = src.shape[0]
    n = hi - lo
    two = 2 * lats
    dst[:feat, at : at + n] = pltpu.roll(src[:, lo - two : hi], lats, 1)[:, two:]
    dst[feat : 2 * feat, at : at + n] = src[:, lo:hi]
    dst[2 * feat :, at : at + n] = pltpu.roll(src[:, lo : hi + two], n + two - lats, 1)[:, :n]


def sum_lats(p, lats):
    chans = p.shape[0] // 3
    n = p.shape[1]
    lat = lat_of(n, lats)
    below = jnp.where(lat == 0, 0.0, pltpu.roll(p[:chans], 1, 1))
    above = jnp.where(lat == lats - 1, 0.0, pltpu.roll(p[2 * chans :], n - 1, 1))
    return p[chans : 2 * chans] + below + above


def folded(v):
    acc = v[:, :128]
    for i in range(1, v.shape[1] // 128):
        acc = acc + v[:, 128 * i : 128 * (i + 1)]
    tile = acc[:8]
    for i in range(1, acc.shape[0] // 8):
        tile = tile + acc[8 * i : 8 * (i + 1)]
    return tile


def chunks(lo, hi, size=256):
    return [(c, min(c + size, hi)) for c in range(lo, hi, size)]


def kernel(
    total, tms, lons, lats,
    *refs,
):
    sources, step, out, costs = refs[:12], refs[12], refs[13], refs[14]
    fg, bg, w1t, b1, w2, b2, mw, bw, cell, chan, val, wt = held = refs[15:27]
    (
        xe, rx, sx, sten, hf, hs, gp, qf, mx, lx, gx, ow, ov, v2, w1s, w1p, v1p, tall, tall1, pp, cg,
        ms, mr, ls, le, ar1, ar2,
        in_sem, halo_send, halo_recv, edge_send, edge_recv, m_send, m_recv, a1_send, a1_recv, a2_send, a2_recv,
    ) = refs[27:]
    subs, own, chans = fg.shape
    feat = w1t.shape[1]
    two = 2 * lats
    lo, hi = two, two + own
    ext = hi + two
    loads = [pltpu.make_async_copy(src, dst, in_sem.at[i]) for i, (src, dst) in enumerate(zip(sources, held))]
    for c in loads:
        c.start()
    t = lax.axis_index("tm")
    l = lax.axis_index("lon")
    tp, tn = lax.rem(t + tms - 1, tms), lax.rem(t + 1, tms)
    ll, lr = lax.rem(l + lons - 1, lons), lax.rem(l + 1, lons)
    lon_peers = [lax.rem(l + d, lons) for d in range(1, lons)]
    tm_peers = [lax.rem(t + d, tms) for d in range(1, tms)]

    barrier = pltpu.get_barrier_semaphore()
    for peer in lon_peers:
        pl.semaphore_signal(barrier, inc=1, device_id=(t, peer), device_id_type=MESH)
    for peer in tm_peers:
        pl.semaphore_signal(barrier, inc=1, device_id=(peer, l), device_id_type=MESH)

    def halo_copies(it):
        src, dst = sx.at[it], rx.at[it]
        parts = (
            (src.at[:, :, own - two :], dst.at[:subs, :, :lo], (t, lr)),
            (src.at[:, :, :two], dst.at[:subs, :, hi:], (t, ll)),
            (src.at[:1], dst.at[subs:, :, lo:hi], (tp, l)),
        )
        return [
            pltpu.make_async_remote_copy(
                src_ref=s, dst_ref=d, send_sem=halo_send.at[it, i], recv_sem=halo_recv.at[it, i],
                device_id=dev, device_id_type=MESH,
            )
            for i, (s, d, dev) in enumerate(parts)
        ]

    def edge_copies(it, s):
        parts = ((slice(own - two, own), slice(0, lo), lr), (slice(0, two), slice(hi, ext), ll))
        return [
            pltpu.make_async_remote_copy(
                src_ref=ls.at[it, s, :, x], dst_ref=le.at[it, s, :, y],
                send_sem=edge_send.at[it, s, i], recv_sem=edge_recv.at[it, s, i],
                device_id=(t, peer), device_id_type=MESH,
            )
            for i, (x, y, peer) in enumerate(parts)
        ]

    loads[0].wait()
    for s in range(subs):
        x = jnp.transpose(fg[s])
        xe[s, :, lo:hi] = x
        sx[0, s] = x.astype(BF16)
    pl.semaphore_wait(barrier, lons - 1 + tms - 1)
    pending = []
    halos = halo_copies(0)
    for c in halos:
        c.start()

    for c in loads[1:]:
        c.wait()

    for a in range(3):
        for b in range(3):
            block = w2[:, (3 * a + b) * feat : (3 * a + b + 1) * feat]
            v2[b * chans : (b + 1) * chans, a * feat : (a + 1) * feat] = block
            at = (3 * (2 - a) + (2 - b)) * chans
            tall[at : at + chans, :] = block.astype(F32)
    tall[9 * chans :, :] = jnp.zeros((tall.shape[0] - 9 * chans, feat), F32)
    w1p[...] = jnp.transpose(tall[...]).astype(BF16)
    tall1[: 9 * chans, :] = w1t[...].astype(F32)
    tall1[9 * chans :, :] = jnp.zeros((tall1.shape[0] - 9 * chans, feat), F32)
    w1s[...] = jnp.transpose(tall1[...]).astype(BF16)
    for a in range(3):
        for b in range(3):
            at = (3 * (2 - a) + (2 - b)) * chans
            v1p[b * chans : (b + 1) * chans, a * feat : (a + 1) * feat] = w1t[at : at + chans, :]
    b1c, b2c, mwc, bwc = column(b1[...]), column(b2[...]), column(mw[...]), column(bw[...])

    fixed = jnp.zeros((), F32)
    nobs = cell.shape[1]
    for s in range(subs):
        weight, value = wt[s : s + 1, :], val[s : s + 1, :]
        fixed = fixed + jnp.sum(weight * value * value)
        at_chan = lax.broadcasted_iota(jnp.int32, (chans, nobs), 0) == chan[s : s + 1, :]
        at_cell = (lax.broadcasted_iota(jnp.int32, (own, nobs), 0) == cell[s : s + 1, :]).astype(F32).astype(BF16)
        rows = []
        for rest in (weight, weight * value):
            for _ in range(3):
                part = rest.astype(BF16).astype(F32)
                rest = rest - part
                rows.append(jnp.where(at_chan, part, 0.0).astype(BF16))
        spread = lax.dot_general(
            jnp.concatenate(rows, axis=0), at_cell, (((1,), (1,)), ((), ())), preferred_element_type=F32
        )
        spread = [spread[i * chans : (i + 1) * chans] for i in range(6)]
        ow[s] = spread[0] + spread[1] + spread[2]
        ov[s] = spread[3] + spread[4] + spread[5]

    starts = (t > 0).astype(F32)
    ends = (t < tms - 1).astype(F32)
    anchor = (t == 0).astype(F32)
    origin = lax.broadcasted_iota(jnp.int32, (8, 128), 0) * 128 + lax.broadcasted_iota(jnp.int32, (8, 128), 1) == 0

    alpha = None
    for it in range(ITERS):
        if it == 0:
            for c in halos:
                c.wait_recv()
        pending += halos
        for s in range(subs + 1):
            for x0, x1 in ((0, lo), (hi, ext)) if s < subs else ((lo, hi),):
                got = rx[it, s, :, x0:x1].astype(F32)
                xe[s, :, x0:x1] = got if it == 0 else xe[s, :, x0:x1] - alpha * got

        edges = {}
        for s in reversed(range(subs)):
            if it == 0:
                im2col(xe[s], sten, lats)
            for c0, c1 in chunks(0, ext):
                if it == 0:
                    pre = jnp.dot(w1s[:, : 9 * chans], sten[:, c0:c1], preferred_element_type=F32) + b1c
                else:
                    pre = pp[s, :, c0:c1] - alpha * cg[s, :, c0:c1]
                if it < ITERS - 1:
                    pp[s, :, c0:c1] = pre
                sq = pre * pre
                half = 0.5 + 0.5 * jnp.tanh(pre * (ROOT + (ROOT * CUBE) * sq))
                hid = pre * half
                hf[:, c0:c1] = hid.astype(BF16)
                gp[s, :, c0:c1] = half + hid * (1.0 - half) * (2.0 * ROOT + (6.0 * ROOT * CUBE) * sq)
            for c0, c1 in chunks(lo, hi):
                at = c0 - lo
                stack_lons(hf, c0, c1, at, hs, lats)
                p = jnp.dot(v2[...], hs[:, at : at + c1 - c0], preferred_element_type=F32)
                mx[s, :, at : at + c1 - c0] = xe[s, :, c0:c1] + sum_lats(p, lats) + b2c
            if s == subs - 1:
                ms[it] = mx[s].astype(BF16)
                m_copy = pltpu.make_async_remote_copy(
                    src_ref=ms.at[it], dst_ref=mr.at[it], send_sem=m_send.at[it], recv_sem=m_recv.at[it],
                    device_id=(tn, l), device_id_type=MESH,
                )
                m_copy.start()
                pending.append(m_copy)

            forcing = (mwc if s < subs - 1 else mwc * ends) * (xe[s + 1, :, lo:hi] - mx[s])
            lx[s + 1, :, lo:hi] = forcing
            ls[it, s] = forcing.astype(BF16)
            edges[s] = edge_copies(it, s)
            for c in edges[s]:
                c.start()
            pending += edges[s]

        norm = jnp.zeros((8, 128), F32)
        cost = jnp.where(origin, fixed, 0.0)
        for s in reversed(range(subs)):
            for c in edges[s]:
                c.wait_recv()
            lx[s + 1, :, :lo] = le[it, s, :, :lo].astype(F32)
            lx[s + 1, :, hi:] = le[it, s, :, hi:].astype(F32)
            im2col(lx[s + 1], sten, lats)
            for c0, c1 in chunks(0, ext):
                z = jnp.dot(w1p[:, : 9 * chans], sten[:, c0:c1], preferred_element_type=F32)
                qf[:, c0:c1] = (gp[s, :, c0:c1] * z).astype(BF16)
            pulled = []
            for c0, c1 in chunks(lo, hi):
                at = c0 - lo
                stack_lons(qf, c0, c1, at, hs, lats)
                p = jnp.dot(v1p[...], hs[:, at : at + c1 - c0], preferred_element_type=F32)
                pulled.append(lx[s + 1, :, c0:c1] + sum_lats(p, lats))
            pulled = jnp.concatenate(pulled, axis=1)
            x = xe[s, :, lo:hi]
            if s > 0:
                forcing = lx[s, :, lo:hi]
                defect = x - mx[s - 1]
            else:
                m_copy.wait_recv()
                defect = x - mr[it].astype(F32)
                forcing = (mwc * starts) * defect
            weighted = ow[s] * x - ov[s]
            cost = cost + folded(forcing * defect + (weighted - ov[s]) * x)
            g = forcing - pulled + weighted
            if s == 0:
                back = jnp.transpose(bg[...])
                departure = x - back
                pull = (bwc * anchor) * departure
                cost = cost + folded(pull * departure)
                g = g + pull
            norm = norm + folded(g * g)
            gx[s] = g
            if it < ITERS - 1:
                sx[it + 1, s] = g.astype(BF16)

        ar1[it, l, :8] = norm
        ar1[it, l, 8:] = cost
        first_phase = [
            pltpu.make_async_remote_copy(
                src_ref=ar1.at[it, l], dst_ref=ar1.at[it, l], send_sem=a1_send.at[it, i], recv_sem=a1_recv.at[it, i],
                device_id=(t, peer), device_id_type=MESH,
            )
            for i, peer in enumerate(lon_peers)
        ]
        for c in first_phase:
            c.start()
        if it < ITERS - 1:
            halos = halo_copies(it + 1)
            for c in halos:
                c.start()
        for c in first_phase:
            c.wait_recv()
        ar2[it, t] = functools.reduce(jnp.add, [ar1[it, i] for i in range(lons)])
        second_phase = [
            pltpu.make_async_remote_copy(
                src_ref=ar2.at[it, t], dst_ref=ar2.at[it, t], send_sem=a2_send.at[it, i], recv_sem=a2_recv.at[it, i],
                device_id=(peer, l), device_id_type=MESH,
            )
            for i, peer in enumerate(tm_peers)
        ]
        for c in second_phase:
            c.start()
        if it < ITERS - 1:
            for c in halos:
                c.wait_recv()
            for s in range(subs):
                left, right = rx[it + 1, s, :, :lo].astype(F32), rx[it + 1, s, :, hi:].astype(F32)
                im2col(jnp.concatenate([left, gx[s], right], axis=1), sten, lats)
                for c0, c1 in chunks(0, ext):
                    cg[s, :, c0:c1] = jnp.dot(
                        w1s[:, : 9 * chans], sten[:, c0:c1], preferred_element_type=F32
                    )
        for c in second_phase:
            c.wait_recv()
        pending += first_phase + second_phase
        both = functools.reduce(jnp.add, [ar2[it, i] for i in range(tms)])
        costs[it] = 0.5 * jnp.sum(both[8:])
        sum_sq = jnp.sum(jnp.sum(both[:8], axis=0, keepdims=True), axis=1, keepdims=True)
        alpha = step[...] / jnp.sqrt(sum_sq / total + 1e-06)
        for s in range(subs):
            x = xe[s, :, lo:hi] - alpha * gx[s]
            if it < ITERS - 1:
                xe[s, :, lo:hi] = x
            else:
                out[s] = jnp.transpose(x)
    for c in pending:
        c.wait_send()


def per_device(fg, bg, w1, b1, w2, b2, mw, bw, cell, chan, val, wt, step):
    subs, band, chans, lats = fg.shape
    feat = w1.shape[0]
    tms, lons = lax.axis_size("tm"), lax.axis_size("lon")
    total = float(subs * tms * band * lons * chans * lats)
    own = band * lats
    ext = own + 4 * lats
    rows = -(-9 * chans // 128) * 128
    vmem = pl.BlockSpec(memory_space=pltpu.VMEM)
    dma = pltpu.SemaphoreType.DMA
    arrays = (
        jnp.swapaxes(fg, 2, 3).reshape(subs, own, chans), jnp.swapaxes(bg, 1, 2).reshape(own, chans),
        w1.T, b1.reshape(1, -1), w2, b2.reshape(1, -1), mw.reshape(1, -1), bw.reshape(1, -1),
        cell, chan, val, wt,
    )
    analysis, costs = pl.pallas_call(
        functools.partial(kernel, total, tms, lons, lats),
        out_shape=(
            jax.ShapeDtypeStruct((subs, own, chans), F32),
            jax.ShapeDtypeStruct((ITERS,), F32),
        ),
        in_specs=[pl.BlockSpec(memory_space=pl.ANY)] * 12 + [vmem],
        out_specs=(vmem, pl.BlockSpec(memory_space=pltpu.SMEM)),
        scratch_shapes=[pltpu.VMEM(v.shape, v.dtype) for v in arrays]
        + [
            pltpu.VMEM((subs + 1, chans, ext), F32),
            pltpu.VMEM((ITERS, subs + 1, chans, ext), BF16),
            pltpu.VMEM((ITERS, subs, chans, own), BF16),
            pltpu.VMEM((9 * chans, ext), BF16),
            pltpu.VMEM((feat, ext), BF16),
            pltpu.VMEM((3 * feat, own), BF16),
            pltpu.VMEM((subs, feat, ext), F32),
            pltpu.VMEM((feat, ext), BF16),
            pltpu.VMEM((subs, chans, own), F32),
            pltpu.VMEM((subs + 1, chans, ext), F32),
            pltpu.VMEM((subs, chans, own), F32),
            pltpu.VMEM((subs, chans, own), F32),
            pltpu.VMEM((subs, chans, own), F32),
            pltpu.VMEM((3 * chans, 3 * feat), BF16),
            pltpu.VMEM((feat, rows), BF16),
            pltpu.VMEM((feat, rows), BF16),
            pltpu.VMEM((3 * chans, 3 * feat), BF16),
            pltpu.VMEM((rows, feat), F32),
            pltpu.VMEM((rows, feat), F32),
            pltpu.VMEM((subs, feat, ext), F32),
            pltpu.VMEM((subs, feat, ext), F32),
            pltpu.VMEM((ITERS, chans, own), BF16),
            pltpu.VMEM((ITERS, chans, own), BF16),
            pltpu.VMEM((ITERS, subs, chans, own), BF16),
            pltpu.VMEM((ITERS, subs, chans, ext), BF16),
            pltpu.VMEM((ITERS, lons, 16, 128), F32),
            pltpu.VMEM((ITERS, tms, 16, 128), F32),
            dma((12,)),
            dma((ITERS, 3)),
            dma((ITERS, 3)),
            dma((ITERS, subs, 2)),
            dma((ITERS, subs, 2)),
            dma((ITERS,)),
            dma((ITERS,)),
            dma((ITERS, lons - 1)),
            dma((ITERS, lons - 1)),
            dma((ITERS, tms - 1)),
            dma((ITERS, tms - 1)),
        ],
        compiler_params=pltpu.CompilerParams(
            collective_id=0, has_side_effects=True, vmem_limit_bytes=60 * 1024 * 1024
        ),
    )(*arrays, step.reshape(1, 1))
    return jnp.swapaxes(analysis.reshape(subs, band, lats, chans), 2, 3), costs


def solution(mesh):
    in_specs = (
        P("tm", "lon", None, None),
        P("lon", None, None),
        P(),
        P(),
        P(),
        P(),
        P(),
        P(),
        P("tm", "lon"),
        P("tm", "lon"),
        P("tm", "lon"),
        P("tm", "lon"),
        P(),
    )
    out_specs = (P("tm", "lon", None, None), P())
    return jax.shard_map(
        per_device, mesh=mesh, in_specs=in_specs, out_specs=out_specs, check_vma=False
    )
```

```python
import functools

import jax
import jax.numpy as jnp
from jax import lax
from jax.experimental import pallas as pl
from jax.experimental.pallas import tpu as pltpu
from jax.sharding import PartitionSpec as P

ITERS = 2
F32 = jnp.float32
BF16 = jnp.bfloat16
MESH = pl.DeviceIdType.MESH
ROOT = 0.7978845608028654
CUBE = 0.044715


def column(row):
    n = row.shape[1]
    eye = lax.broadcasted_iota(jnp.int32, (n, n), 0) == lax.broadcasted_iota(jnp.int32, (n, n), 1)
    return jnp.sum(jnp.where(eye, row, 0.0), axis=1, keepdims=True)


def lat_of(n, lats):
    return lax.broadcasted_iota(jnp.int32, (1, n), 1) % lats


def im2col(x, dst, lats):
    chans, n = x.shape
    lat = lat_of(n, lats)
    below = jnp.where(lat == 0, 0.0, pltpu.roll(x, 1, 1))
    above = jnp.where(lat == lats - 1, 0.0, pltpu.roll(x, n - 1, 1))
    for b, wide in enumerate((below, x, above)):
        v = wide.astype(BF16)
        for a, w in enumerate((pltpu.roll(v, lats, 1), v, pltpu.roll(v, n - lats, 1))):
            at = (3 * a + b) * chans
            dst[at : at + chans, :n] = w


def stack_lons(src, lo, hi, at, dst, lats):
    feat = src.shape[0]
    n = hi - lo
    two = 2 * lats
    dst[:feat, at : at + n] = pltpu.roll(src[:, lo - two : hi], lats, 1)[:, two:]
    dst[feat : 2 * feat, at : at + n] = src[:, lo:hi]
    dst[2 * feat :, at : at + n] = pltpu.roll(src[:, lo : hi + two], n + two - lats, 1)[:, :n]


def sum_lats(p, lats):
    chans = p.shape[0] // 3
    n = p.shape[1]
    lat = lat_of(n, lats)
    below = jnp.where(lat == 0, 0.0, pltpu.roll(p[:chans], 1, 1))
    above = jnp.where(lat == lats - 1, 0.0, pltpu.roll(p[2 * chans :], n - 1, 1))
    return p[chans : 2 * chans] + below + above


def folded(v):
    acc = v[:, :128]
    for i in range(1, v.shape[1] // 128):
        acc = acc + v[:, 128 * i : 128 * (i + 1)]
    tile = acc[:8]
    for i in range(1, acc.shape[0] // 8):
        tile = tile + acc[8 * i : 8 * (i + 1)]
    return tile


def chunks(lo, hi, size=256):
    return [(c, min(c + size, hi)) for c in range(lo, hi, size)]


def kernel(
    total, tms, lons, lats,
    *refs,
):
    sources, step, out, costs = refs[:12], refs[12], refs[13], refs[14]
    fg, bg, w1t, b1, w2, b2, mw, bw, cell, chan, val, wt = held = refs[15:27]
    (
        xe, rx, sx, sten, hf, hs, gp, qf, mx, lx, gx, ow, ov, v2, w1s, w1p, v1p, tall, tall1, pp, cg,
        ms, mr, ls, le, ar1, ar2,
        in_sem, halo_send, halo_recv, edge_send, edge_recv, m_send, m_recv, a1_send, a1_recv, a2_send, a2_recv,
    ) = refs[27:]
    subs, own, chans = fg.shape
    feat = w1t.shape[1]
    two = 2 * lats
    lo, hi = two, two + own
    ext = hi + two
    loads = [pltpu.make_async_copy(src, dst, in_sem.at[i]) for i, (src, dst) in enumerate(zip(sources, held))]
    for c in loads:
        c.start()
    t = lax.axis_index("tm")
    l = lax.axis_index("lon")
    tp, tn = lax.rem(t + tms - 1, tms), lax.rem(t + 1, tms)
    ll, lr = lax.rem(l + lons - 1, lons), lax.rem(l + 1, lons)
    lon_peers = [lax.rem(l + d, lons) for d in range(1, lons)]
    tm_peers = [lax.rem(t + d, tms) for d in range(1, tms)]

    barrier = pltpu.get_barrier_semaphore()
    for peer in lon_peers:
        pl.semaphore_signal(barrier, inc=1, device_id=(t, peer), device_id_type=MESH)
    for peer in tm_peers:
        pl.semaphore_signal(barrier, inc=1, device_id=(peer, l), device_id_type=MESH)

    def halo_copies(it):
        src, dst = sx.at[it], rx.at[it]
        parts = (
            (src.at[:, :, own - two :], dst.at[:subs, :, :lo], (t, lr)),
            (src.at[:, :, :two], dst.at[:subs, :, hi:], (t, ll)),
            (src.at[:1], dst.at[subs:, :, lo:hi], (tp, l)),
        )
        return [
            pltpu.make_async_remote_copy(
                src_ref=s, dst_ref=d, send_sem=halo_send.at[it, i], recv_sem=halo_recv.at[it, i],
                device_id=dev, device_id_type=MESH,
            )
            for i, (s, d, dev) in enumerate(parts)
        ]

    def edge_copies(it, s):
        parts = ((slice(own - two, own), slice(0, lo), lr), (slice(0, two), slice(hi, ext), ll))
        return [
            pltpu.make_async_remote_copy(
                src_ref=ls.at[it, s, :, x], dst_ref=le.at[it, s, :, y],
                send_sem=edge_send.at[it, s, i], recv_sem=edge_recv.at[it, s, i],
                device_id=(t, peer), device_id_type=MESH,
            )
            for i, (x, y, peer) in enumerate(parts)
        ]

    loads[0].wait()
    for s in range(subs):
        x = jnp.transpose(fg[s])
        xe[s, :, lo:hi] = x
        sx[0, s] = x.astype(BF16)
    pl.semaphore_wait(barrier, lons - 1 + tms - 1)
    pending = []
    halos = halo_copies(0)
    for c in halos:
        c.start()

    for c in loads[1:]:
        c.wait()

    for a in range(3):
        for b in range(3):
            block = w2[:, (3 * a + b) * feat : (3 * a + b + 1) * feat]
            v2[b * chans : (b + 1) * chans, a * feat : (a + 1) * feat] = block
            at = (3 * (2 - a) + (2 - b)) * chans
            tall[at : at + chans, :] = block.astype(F32)
    tall[9 * chans :, :] = jnp.zeros((tall.shape[0] - 9 * chans, feat), F32)
    w1p[...] = jnp.transpose(tall[...]).astype(BF16)
    tall1[: 9 * chans, :] = w1t[...].astype(F32)
    tall1[9 * chans :, :] = jnp.zeros((tall1.shape[0] - 9 * chans, feat), F32)
    w1s[...] = jnp.transpose(tall1[...]).astype(BF16)
    for a in range(3):
        for b in range(3):
            at = (3 * (2 - a) + (2 - b)) * chans
            v1p[b * chans : (b + 1) * chans, a * feat : (a + 1) * feat] = w1t[at : at + chans, :]
    b1c, b2c, mwc, bwc = column(b1[...]), column(b2[...]), column(mw[...]), column(bw[...])

    fixed = jnp.zeros((), F32)
    nobs = cell.shape[1]
    for s in range(subs):
        weight, value = wt[s : s + 1, :], val[s : s + 1, :]
        fixed = fixed + jnp.sum(weight * value * value)
        at_chan = lax.broadcasted_iota(jnp.int32, (chans, nobs), 0) == chan[s : s + 1, :]
        at_cell = (lax.broadcasted_iota(jnp.int32, (own, nobs), 0) == cell[s : s + 1, :]).astype(F32).astype(BF16)
        rows = []
        for rest in (weight, weight * value):
            for _ in range(3):
                part = rest.astype(BF16).astype(F32)
                rest = rest - part
                rows.append(jnp.where(at_chan, part, 0.0).astype(BF16))
        spread = lax.dot_general(
            jnp.concatenate(rows, axis=0), at_cell, (((1,), (1,)), ((), ())), preferred_element_type=F32
        )
        spread = [spread[i * chans : (i + 1) * chans] for i in range(6)]
        ow[s] = spread[0] + spread[1] + spread[2]
        ov[s] = spread[3] + spread[4] + spread[5]

    starts = (t > 0).astype(F32)
    ends = (t < tms - 1).astype(F32)
    anchor = (t == 0).astype(F32)
    origin = lax.broadcasted_iota(jnp.int32, (8, 128), 0) * 128 + lax.broadcasted_iota(jnp.int32, (8, 128), 1) == 0

    alpha = None
    for it in range(ITERS):
        if it == 0:
            for c in halos:
                c.wait_recv()
        pending += halos
        for s in range(subs + 1):
            for x0, x1 in ((0, lo), (hi, ext)) if s < subs else ((lo, hi),):
                got = rx[it, s, :, x0:x1].astype(F32)
                xe[s, :, x0:x1] = got if it == 0 else xe[s, :, x0:x1] - alpha * got

        edges = {}
        for s in reversed(range(subs)):
            if it == 0:
                im2col(xe[s], sten, lats)
            for c0, c1 in chunks(0, ext):
                if it == 0:
                    pre = jnp.dot(w1s[:, : 9 * chans], sten[:, c0:c1], preferred_element_type=F32) + b1c
                else:
                    pre = pp[s, :, c0:c1] - alpha * cg[s, :, c0:c1]
                if it < ITERS - 1:
                    pp[s, :, c0:c1] = pre
                sq = pre * pre
                half = 0.5 + 0.5 * jnp.tanh(pre * (ROOT + (ROOT * CUBE) * sq))
                hid = pre * half
                hf[:, c0:c1] = hid.astype(BF16)
                gp[s, :, c0:c1] = half + hid * (1.0 - half) * (2.0 * ROOT + (6.0 * ROOT * CUBE) * sq)
            for c0, c1 in chunks(lo, hi):
                at = c0 - lo
                stack_lons(hf, c0, c1, at, hs, lats)
                p = jnp.dot(v2[...], hs[:, at : at + c1 - c0], preferred_element_type=F32)
                mx[s, :, at : at + c1 - c0] = xe[s, :, c0:c1] + sum_lats(p, lats) + b2c
            if s == subs - 1:
                ms[it] = mx[s].astype(BF16)
                m_copy = pltpu.make_async_remote_copy(
                    src_ref=ms.at[it], dst_ref=mr.at[it], send_sem=m_send.at[it], recv_sem=m_recv.at[it],
                    device_id=(tn, l), device_id_type=MESH,
                )
                m_copy.start()
                pending.append(m_copy)

            forcing = (mwc if s < subs - 1 else mwc * ends) * (xe[s + 1, :, lo:hi] - mx[s])
            lx[s + 1, :, lo:hi] = forcing
            ls[it, s] = forcing.astype(BF16)
            edges[s] = edge_copies(it, s)
            for c in edges[s]:
                c.start()
            pending += edges[s]

        norm = jnp.zeros((8, 128), F32)
        cost = jnp.where(origin, fixed, 0.0)
        for s in reversed(range(subs)):
            for c in edges[s]:
                c.wait_recv()
            lx[s + 1, :, :lo] = le[it, s, :, :lo].astype(F32)
            lx[s + 1, :, hi:] = le[it, s, :, hi:].astype(F32)
            im2col(lx[s + 1], sten, lats)
            for c0, c1 in chunks(0, ext):
                z = jnp.dot(w1p[:, : 9 * chans], sten[:, c0:c1], preferred_element_type=F32)
                qf[:, c0:c1] = (gp[s, :, c0:c1] * z).astype(BF16)
            pulled = []
            for c0, c1 in chunks(lo, hi):
                at = c0 - lo
                stack_lons(qf, c0, c1, at, hs, lats)
                p = jnp.dot(v1p[...], hs[:, at : at + c1 - c0], preferred_element_type=F32)
                pulled.append(lx[s + 1, :, c0:c1] + sum_lats(p, lats))
            pulled = jnp.concatenate(pulled, axis=1)
            x = xe[s, :, lo:hi]
            if s > 0:
                forcing = lx[s, :, lo:hi]
                defect = x - mx[s - 1]
            else:
                m_copy.wait_recv()
                defect = x - mr[it].astype(F32)
                forcing = (mwc * starts) * defect
            weighted = ow[s] * x - ov[s]
            cost = cost + folded(forcing * defect + (weighted - ov[s]) * x)
            g = forcing - pulled + weighted
            if s == 0:
                back = jnp.transpose(bg[...])
                departure = x - back
                pull = (bwc * anchor) * departure
                cost = cost + folded(pull * departure)
                g = g + pull
            norm = norm + folded(g * g)
            gx[s] = g
            if it < ITERS - 1:
                sx[it + 1, s] = g.astype(BF16)

        norm, cost = jnp.sum(norm, axis=0, keepdims=True), jnp.sum(cost, axis=0, keepdims=True)
        low = lax.broadcasted_iota(jnp.int32, (1, 128), 1) < 64
        fold = lambda v: v + jnp.concatenate([v[:, 64:], v[:, :64]], axis=1)
        ar1[it, l] = jnp.where(low, fold(norm), fold(cost))
        first_phase = [
            pltpu.make_async_remote_copy(
                src_ref=ar1.at[it, l], dst_ref=ar1.at[it, l], send_sem=a1_send.at[it, i], recv_sem=a1_recv.at[it, i],
                device_id=(t, peer), device_id_type=MESH,
            )
            for i, peer in enumerate(lon_peers)
        ]
        for c in first_phase:
            c.start()
        if it < ITERS - 1:
            halos = halo_copies(it + 1)
            for c in halos:
                c.start()
        for c in first_phase:
            c.wait_recv()
        ar2[it, t] = functools.reduce(jnp.add, [ar1[it, i] for i in range(lons)])
        second_phase = [
            pltpu.make_async_remote_copy(
                src_ref=ar2.at[it, t], dst_ref=ar2.at[it, t], send_sem=a2_send.at[it, i], recv_sem=a2_recv.at[it, i],
                device_id=(peer, l), device_id_type=MESH,
            )
            for i, peer in enumerate(tm_peers)
        ]
        for c in second_phase:
            c.start()
        if it < ITERS - 1:
            for c in halos:
                c.wait_recv()
            for s in range(subs):
                left, right = rx[it + 1, s, :, :lo].astype(F32), rx[it + 1, s, :, hi:].astype(F32)
                im2col(jnp.concatenate([left, gx[s], right], axis=1), sten, lats)
                for c0, c1 in chunks(0, ext):
                    cg[s, :, c0:c1] = jnp.dot(
                        w1s[:, : 9 * chans], sten[:, c0:c1], preferred_element_type=F32
                    )
        for c in second_phase:
            c.wait_recv()
        pending += first_phase + second_phase
        both = functools.reduce(jnp.add, [ar2[it, i] for i in range(tms)])
        costs[it] = 0.5 * jnp.sum(jnp.where(low, 0.0, both))
        sum_sq = jnp.sum(jnp.where(low, both, 0.0), axis=1, keepdims=True)
        alpha = step[...] / jnp.sqrt(sum_sq / total + 1e-06)
        for s in range(subs):
            x = xe[s, :, lo:hi] - alpha * gx[s]
            if it < ITERS - 1:
                xe[s, :, lo:hi] = x
            else:
                out[s] = jnp.transpose(x)
    for c in pending:
        c.wait_send()


def per_device(fg, bg, w1, b1, w2, b2, mw, bw, cell, chan, val, wt, step):
    subs, band, chans, lats = fg.shape
    feat = w1.shape[0]
    tms, lons = lax.axis_size("tm"), lax.axis_size("lon")
    total = float(subs * tms * band * lons * chans * lats)
    own = band * lats
    ext = own + 4 * lats
    rows = -(-9 * chans // 128) * 128
    vmem = pl.BlockSpec(memory_space=pltpu.VMEM)
    dma = pltpu.SemaphoreType.DMA
    arrays = (
        jnp.swapaxes(fg, 2, 3).reshape(subs, own, chans), jnp.swapaxes(bg, 1, 2).reshape(own, chans),
        w1.T, b1.reshape(1, -1), w2, b2.reshape(1, -1), mw.reshape(1, -1), bw.reshape(1, -1),
        cell, chan, val, wt,
    )
    analysis, costs = pl.pallas_call(
        functools.partial(kernel, total, tms, lons, lats),
        out_shape=(
            jax.ShapeDtypeStruct((subs, own, chans), F32),
            jax.ShapeDtypeStruct((ITERS,), F32),
        ),
        in_specs=[pl.BlockSpec(memory_space=pl.ANY)] * 12 + [vmem],
        out_specs=(vmem, pl.BlockSpec(memory_space=pltpu.SMEM)),
        scratch_shapes=[pltpu.VMEM(v.shape, v.dtype) for v in arrays]
        + [
            pltpu.VMEM((subs + 1, chans, ext), F32),
            pltpu.VMEM((ITERS, subs + 1, chans, ext), BF16),
            pltpu.VMEM((ITERS, subs, chans, own), BF16),
            pltpu.VMEM((9 * chans, ext), BF16),
            pltpu.VMEM((feat, ext), BF16),
            pltpu.VMEM((3 * feat, own), BF16),
            pltpu.VMEM((subs, feat, ext), F32),
            pltpu.VMEM((feat, ext), BF16),
            pltpu.VMEM((subs, chans, own), F32),
            pltpu.VMEM((subs + 1, chans, ext), F32),
            pltpu.VMEM((subs, chans, own), F32),
            pltpu.VMEM((subs, chans, own), F32),
            pltpu.VMEM((subs, chans, own), F32),
            pltpu.VMEM((3 * chans, 3 * feat), BF16),
            pltpu.VMEM((feat, rows), BF16),
            pltpu.VMEM((feat, rows), BF16),
            pltpu.VMEM((3 * chans, 3 * feat), BF16),
            pltpu.VMEM((rows, feat), F32),
            pltpu.VMEM((rows, feat), F32),
            pltpu.VMEM((subs, feat, ext), F32),
            pltpu.VMEM((subs, feat, ext), F32),
            pltpu.VMEM((ITERS, chans, own), BF16),
            pltpu.VMEM((ITERS, chans, own), BF16),
            pltpu.VMEM((ITERS, subs, chans, own), BF16),
            pltpu.VMEM((ITERS, subs, chans, ext), BF16),
            pltpu.VMEM((ITERS, lons, 1, 128), F32),
            pltpu.VMEM((ITERS, tms, 1, 128), F32),
            dma((12,)),
            dma((ITERS, 3)),
            dma((ITERS, 3)),
            dma((ITERS, subs, 2)),
            dma((ITERS, subs, 2)),
            dma((ITERS,)),
            dma((ITERS,)),
            dma((ITERS, lons - 1)),
            dma((ITERS, lons - 1)),
            dma((ITERS, tms - 1)),
            dma((ITERS, tms - 1)),
        ],
        compiler_params=pltpu.CompilerParams(
            collective_id=0, has_side_effects=True, vmem_limit_bytes=60 * 1024 * 1024
        ),
    )(*arrays, step.reshape(1, 1))
    return jnp.swapaxes(analysis.reshape(subs, band, lats, chans), 2, 3), costs


def solution(mesh):
    in_specs = (
        P("tm", "lon", None, None),
        P("lon", None, None),
        P(),
        P(),
        P(),
        P(),
        P(),
        P(),
        P("tm", "lon"),
        P("tm", "lon"),
        P("tm", "lon"),
        P("tm", "lon"),
        P(),
    )
    out_specs = (P("tm", "lon", None, None), P())
    return jax.shard_map(
        per_device, mesh=mesh, in_specs=in_specs, out_specs=out_specs, check_vma=False
    )
```
